256 devices in a mesh: doc: 2 (over core), seq: 128 (over z, x, y).
Axes of the slice: x: 4, y: 4, z: 8, core: 2. Of those that a mesh axis runs over, the one named last changes fastest.
Arguments:
- tokens: bfloat16 [2, 128, 128, 768], P('doc', 'seq'), may hold values from -6 to 6
- norm_gain: float32 [768], replicated, may hold values from 0.1 to 1.9
- proj_weight: bfloat16 [768, 2304], replicated, may hold values from -0.21875 to 0.21875
- out_weight: bfloat16 [768, 768], replicated, may hold values from -0.21875 to 0.21875
- filter_spectrum: float32 [2, 768, 128, 128], P(None, 'seq'), may hold values from -6 to 6
- span_start: int32 [2, 128], P('doc'), may hold values from 0 to 16128, as said below
- span_end: int32 [2, 128], P('doc'), may hold values from 256 to 16384, as said below
- queries: bfloat16 [512, 768], P(('doc', 'seq')), may hold values from -6 to 6
- labels: int32 [512], P(('doc', 'seq')), may hold values from 0 to 255
Outputs:
- layer_out: bfloat16 [2, 128, 128, 768], P('doc', 'seq')
- passage_grad: float32 [2, 128, 768], P('doc', 'seq')
The draws below stay inside these ranges and needn't reach their ends.
Inputs may be any that keep to these rules, and one draw needn't show every extreme that they name: A passage covers tokens span_start to span_end - 1 of its document; span_end - span_start is at least 256 and at most 8192; in every document some passage of length 256 starts at 0 and another of that length ends at 16384. Passages may intersect. `span_end`: see span_start.
All inputs are finite; a program needn't handle non-finite values.
Results may differ from the reference program's by a relative error of at most 0.0085.
Values may be sent and summed in bfloat16 or wider, within the bound.
A program may use at most 64 MiB of HBM per device.

```python
import jax
import jax.numpy as jnp
from jax import lax

D = 768
TOK_DEV = 128
DOCS = 2
SHARDS = 128
TOKENS = 16384
SPANS = 128
QUERIES = 512


def span_bounds(key):
    base_key = jax.random.fold_in(key, 4242)
    key_length, key_start, key_first, key_shift = jax.random.split(base_key, 4)
    span_length = jax.random.randint(key_length, (DOCS, SPANS), TOKENS // 64, TOKENS // 2 + 1)
    raw_start = jax.random.randint(key_start, (DOCS, SPANS), 0, TOKENS)
    first_slot = jax.random.randint(key_first, (DOCS, 1), 0, SPANS)
    final_slot = (first_slot + jax.random.randint(key_shift, (DOCS, 1), 1, SPANS)) % SPANS
    slot_index = lax.broadcasted_iota(jnp.int32, (DOCS, SPANS), 1)
    edge_slot = (slot_index == first_slot) | (slot_index == final_slot)
    span_length = jnp.where(edge_slot, TOKENS // 64, span_length)
    start_pos = raw_start % (TOKENS - span_length + 1)
    start_pos = jnp.where(slot_index == first_slot, 0, start_pos)
    start_pos = jnp.where(slot_index == final_slot, TOKENS - span_length, start_pos)
    return (start_pos.astype(jnp.int32), (start_pos + span_length).astype(jnp.int32))


def draw_span_start(key, part):
    return span_bounds(key)[0]


def draw_span_end(key, part):
    return span_bounds(key)[1]


def touch_ends(drawn, stream_key, least, largest):
    longest = drawn.shape.index(max(drawn.shape))
    spots = []
    for shift in (0, 1):
        where = [jax.random.randint(jax.random.fold_in(stream_key, axis), (), 0, length) for axis, length in enumerate(drawn.shape)]
        where[longest] = (where[longest] + shift) % drawn.shape[longest]
        spots.append(tuple(where))
    return drawn.at[spots[0]].set(least).at[spots[1]].set(largest)


def level_of(stream_key, shape, cuts, smallest, high):
    def one(dim, parts):
        draws = jax.random.uniform(jax.random.fold_in(jax.random.fold_in(stream_key, 6), dim), (parts,), jnp.float32, smallest / len(cuts), high / len(cuts))
        return jnp.repeat(jnp.exp(draws), shape[dim] // parts).reshape((-1,) + (1,) * (len(shape) - dim - 1))

    loudness = one(*cuts[0])
    for cut in cuts[1:]:
        loudness = loudness * one(*cut)
    return loudness


def gaussian(key, extent, spread, most, cuts=(), held_as=jnp.bfloat16):
    level = level_of(key, extent, cuts, -0.22, 0.18) if cuts else 1.0
    values = jax.random.normal(key, extent, jnp.float32) * spread * level
    return jnp.minimum(jnp.maximum(values, -most), most).astype(held_as)


def setup_inputs(seed: int = 0) -> dict:
    arg_keys = jax.random.split(jax.random.key(seed), 10)
    return {
        "tokens": gaussian(arg_keys[0], (DOCS, SHARDS, TOK_DEV, D), 1.0, 6.0, ((0, 2), (1, 128))),
        "norm_gain": jnp.clip(1.0 + 0.18 * jax.random.normal(arg_keys[1], (D,), jnp.float32), 0.1, 1.9),
        "proj_weight": gaussian(arg_keys[2], (D, 3 * D), D ** -0.5, 0.21875),
        "out_weight": gaussian(arg_keys[3], (D, D), D ** -0.5, 0.21875),
        "filter_spectrum": gaussian(arg_keys[4], (2, D, TOK_DEV, SHARDS), 0.7, 6.0, ((1, 128),), jnp.float32),
        "span_start": draw_span_start(jax.random.fold_in(arg_keys[9], 71), 0),
        "span_end": draw_span_end(jax.random.fold_in(arg_keys[9], 71), 0),
        "queries": gaussian(arg_keys[7], (QUERIES, D), 1.0, 6.0, ((0, 256),)),
        "labels": touch_ends(jax.random.randint(arg_keys[8], (QUERIES,), 0, DOCS * SPANS), jax.random.fold_in(arg_keys[8], 1), 0, (DOCS * SPANS) - 1).astype(jnp.int32),
    }


norm_epsilon = 1e-06
logit_scale = 10.0
logit_offset = -4.0
top_precision = lax.Precision.HIGHEST

def unitize(matrix):
    inv_norm = lax.rsqrt(lax.optimization_barrier(jnp.sum(matrix * matrix, axis=1, keepdims=True)) + norm_epsilon)
    return (matrix * inv_norm, inv_norm)

def mix_document(doc_tokens, norm_gain, proj_weight, out_weight, filter_spectrum):
    natural = jnp.transpose(doc_tokens, (1, 0, 2)).reshape(TOKENS, D)
    wide_rows = natural.astype(jnp.float32)
    rms_scale = lax.rsqrt(lax.optimization_barrier(jnp.mean(wide_rows * wide_rows, axis=1, keepdims=True)) + norm_epsilon)
    normed = (wide_rows * rms_scale * norm_gain).astype(jnp.bfloat16)
    gate_first = jnp.dot(normed, proj_weight[:, :D], preferred_element_type=jnp.float32)
    values = jnp.dot(normed, proj_weight[:, D:2 * D], preferred_element_type=jnp.float32)
    signal = gate_first * values
    response_real = jnp.transpose(filter_spectrum[0], (2, 1, 0)).reshape(TOKENS, D)
    response_imag = jnp.transpose(filter_spectrum[1], (2, 1, 0)).reshape(TOKENS, D)
    transformed = jnp.fft.fft(signal, axis=0)
    filtered = transformed * lax.complex(response_real, response_imag)
    conv_out = jnp.real(jnp.fft.ifft(filtered, axis=0))
    gate_second = jnp.dot(normed, proj_weight[:, 2 * D:], preferred_element_type=jnp.float32)
    gated_rows = (gate_second * conv_out).astype(jnp.bfloat16)
    layer_rows = (jnp.dot(gated_rows, out_weight, preferred_element_type=jnp.float32) + wide_rows).astype(jnp.bfloat16)
    return layer_rows

def pool_document(layer_rows, starts, ends):
    position = lax.broadcasted_iota(jnp.int32, (1, TOKENS), 1)
    member = ((position >= starts[:, None]) & (position < ends[:, None])).astype(jnp.bfloat16)
    span_sum = jnp.dot(member, layer_rows, preferred_element_type=jnp.float32)
    counts = (ends - starts).astype(jnp.float32)[:, None]
    return span_sum / counts

def reference(tokens, norm_gain, proj_weight, out_weight, filter_spectrum, span_start, span_end, queries, labels):
    outputs = []
    pooled_all = []
    for doc_number in range(DOCS):
        layer_rows = mix_document(tokens[doc_number], norm_gain, proj_weight, out_weight, filter_spectrum)
        pooled_all.append(pool_document(layer_rows, span_start[doc_number], span_end[doc_number]))
        outputs.append(jnp.transpose(layer_rows.reshape(TOK_DEV, SHARDS, D), (1, 0, 2)))
    layer_out = jnp.stack(outputs, axis=0)
    pooled = jnp.concatenate(pooled_all, axis=0)
    unit_rows, inv_norm = unitize(pooled)
    query_unit, query_inv = unitize(queries.astype(jnp.float32))
    logits = logit_scale * jnp.dot(query_unit, unit_rows.T, precision=top_precision) + logit_offset
    target = lax.broadcasted_iota(jnp.int32, logits.shape, 1)
    label_sign = jnp.where(labels[:, None] == target, 1.0, -1.0).astype(jnp.float32)
    weight = -label_sign * jax.nn.sigmoid(-label_sign * logits)
    unit_grad = logit_scale * jnp.dot(weight.T, query_unit, precision=top_precision)
    radial = lax.optimization_barrier(jnp.sum(unit_rows * unit_grad, axis=1, keepdims=True))
    passage_grad = inv_norm * (unit_grad - unit_rows * radial)
    return (layer_out, passage_grad.reshape(DOCS, SPANS, D))
```

```python
import functools
import math

import jax
import jax.numpy as jnp
import ml_dtypes
import numpy as np
from jax import lax
from jax.experimental import pallas as pl
from jax.experimental.pallas import tpu as pltpu
from jax.sharding import Mesh
from jax.sharding import PartitionSpec as P

SEQ = ("seq_0", "seq_1", "seq_2")
DOC_SEQ = ("doc", "seq_0", "seq_1", "seq_2")
MESH = pl.DeviceIdType.MESH

NZ, NX, NY = 8, 4, 4
SHARDS = 128
TOK = 128
D = 768
CH = 6
N = TOK * SHARDS
QW = D + 128
EPS = 1e-06
SCALE = 10.0
OFFSET = -4.0
F32 = jnp.float32
BF16 = jnp.bfloat16


def split_table(table):
    high = table.astype(ml_dtypes.bfloat16)
    low = (table - high.astype(np.float64)).astype(ml_dtypes.bfloat16)
    return high, low


def tables():
    index = np.arange(128)
    angle = 2.0 * math.pi * ((index[:, None] * index[None, :]) % 128) / 128
    cosine, sine = np.cos(angle), np.sin(angle)
    first = np.stack(split_table(np.concatenate([cosine, -sine], axis=1)))
    first = first.reshape(256, 256)
    second = np.stack(split_table(np.block([[cosine, sine], [-sine, cosine]])))
    third = np.stack(split_table(np.block([[cosine, -sine], [sine, cosine]])))
    fourth = np.stack(split_table(np.concatenate([cosine, -sine], axis=0) / N))
    twist = 2.0 * math.pi * (index[:, None] * index[None, :]) / N
    twist = np.stack([np.cos(twist), np.sin(twist)]).astype(np.float32)
    spread = np.zeros((512, 384), np.float32)
    for slot in range(64):
        for row in range(CH):
            spread[8 * slot + row, CH * slot + row] = 1.0
    spread = spread.astype(ml_dtypes.bfloat16)
    return first, second, third, fourth, twist, twist[:, :, None, :], spread


def dot(a, b):
    return jnp.dot(a, b, preferred_element_type=F32)


def halves(value):
    high = value.astype(BF16)
    low = (value - high.astype(F32)).astype(BF16)
    return high, low


def kernel(
    tok_ref, gain_ref, pw_hbm, ow_hbm, filt_hbm, start_ref, end_ref, q_ref, lab_ref,
    f1_ref, f2_ref, f3_ref, f4_ref, tw_ref, twx_ref, spread_ref,
    out_ref, grad_ref,
    pw, ow, filt, wpad, filt_t,
    send_s, send_g, recv_s, recv_g, send_2, recv_2,
    a_re, a_im, conv_ref,
    qz, qx, qf,
    p0, ry, p1, rx, p2, rz,
    load_sem, a2a_send, a2a_recv, q_send, q_recv, t_send, t_recv,
):
    d = lax.axis_index("doc")
    z = lax.axis_index("seq_0")
    x = lax.axis_index("seq_1")
    y = lax.axis_index("seq_2")
    me = z * 16 + x * 4 + y

    loads = [
        pltpu.make_async_copy(pw_hbm.at[:, pl.ds(D * part, D)], pw.at[part], load_sem.at[part])
        for part in range(3)
    ]
    loads.append(pltpu.make_async_copy(ow_hbm, ow, load_sem.at[3]))
    loads.append(pltpu.make_async_copy(filt_hbm, filt, load_sem.at[4]))
    for load in loads:
        load.start()

    def place(peer):
        return (d, lax.div(peer, 16), lax.rem(lax.div(peer, 4), 4), lax.rem(peer, 4))

    barrier = pltpu.get_barrier_semaphore()

    def greet(step, carry):
        peer = lax.rem(me + step, SHARDS)
        pl.semaphore_signal(barrier, inc=1, device_id=place(peer), device_id_type=MESH)
        return carry

    lax.fori_loop(1, SHARDS, greet, 0)
    pl.semaphore_signal(barrier, inc=1, device_id=(1 - d, z, x, y), device_id_type=MESH)

    start_row = start_ref[...].astype(F32)
    end_row = end_ref[...].astype(F32)
    row_id = lax.broadcasted_iota(jnp.int32, (128, 128), 0)
    lane_id = lax.broadcasted_iota(jnp.int32, (128, 128), 1)
    wanted = ((row_id & 7) << 4) | (((row_id >> 3) & 3) << 2) | (row_id >> 5)
    pick = lane_id == wanted
    start_col = jnp.sum(jnp.where(pick, start_row, 0.0), axis=1, keepdims=True)
    end_col = jnp.sum(jnp.where(pick, end_row, 0.0), axis=1, keepdims=True)
    position = (lane_id * SHARDS + me).astype(F32)
    member = jnp.where((position >= start_col) & (position < end_col), 1.0, 0.0).astype(BF16)
    tokens = tok_ref[...]
    p0[...] = dot(member, tokens).reshape(NY, 32, D)
    ry[y] = p0[y]

    qz[z, :, pl.ds(0, D)] = q_ref[...].astype(F32)
    label_row = lax.broadcasted_iota(jnp.int32, (2, 128), 0)
    qz[z, :, pl.ds(D, 128)] = jnp.where(label_row == 0, lab_ref[0], lab_ref[1]).astype(F32)

    wide = tokens.astype(F32)
    rms = lax.rsqrt(jnp.mean(wide * wide, axis=1, keepdims=True) + EPS)
    normed = (wide * rms * gain_ref[...]).astype(BF16)

    pl.semaphore_wait(barrier, SHARDS)

    def q_copy(src, dst, slot, dev):
        return pltpu.make_async_remote_copy(
            src_ref=src, dst_ref=dst, send_sem=q_send.at[slot], recv_sem=q_recv.at[slot],
            device_id=dev, device_id_type=MESH,
        )

    def t_copy(src, dst, slot, dev):
        return pltpu.make_async_remote_copy(
            src_ref=src, dst_ref=dst, send_sem=t_send.at[slot], recv_sem=t_recv.at[slot],
            device_id=dev, device_id_type=MESH,
        )

    q_z = [q_copy(qz.at[z], qz.at[z], k, (d, lax.rem(z + k, NZ), x, y)) for k in range(1, NZ)]
    t_y = [t_copy(p0.at[lax.rem(y + k, NY)], ry.at[y], k, (d, z, x, lax.rem(y + k, NY))) for k in range(1, NY)]
    for copy in q_z:
        copy.start()

    loads[0].wait()
    loads[1].wait()
    signal = (dot(normed, pw[0]) * dot(normed, pw[1])).astype(BF16)
    contract = (((1,), (1,)), ((), ()))

    def spread_out(value, target):
        for half in range(2):
            part = lax.dot_general(
                spread_ref[...], value[:, 384 * half : 384 * (half + 1)], contract,
                preferred_element_type=F32,
            )
            target[pl.ds(64 * half, 64)] = part.reshape(64, 8, 128).astype(BF16)

    spread_out(signal, send_s)
    recv_s[me] = send_s[me]

    def a2a(src, dst, slot):
        def step(k, carry):
            peer = lax.rem(me + k, SHARDS)
            pltpu.make_async_remote_copy(
                src_ref=src.at[peer], dst_ref=dst.at[me],
                send_sem=a2a_send.at[slot], recv_sem=a2a_recv.at[slot],
                device_id=place(peer), device_id_type=MESH,
            ).start()
            return carry

        lax.fori_loop(1, SHARDS, step, 0)

    def a2a_all(src, dst, slot):
        return pltpu.make_async_remote_copy(
            src_ref=src.at[pl.ds(0, SHARDS - 1)], dst_ref=dst.at[pl.ds(0, SHARDS - 1)],
            send_sem=a2a_send.at[slot], recv_sem=a2a_recv.at[slot],
            device_id=place(lax.rem(me + 1, SHARDS)), device_id_type=MESH,
        )

    a2a(send_s, recv_s, 0)

    loads[2].wait()
    gate = dot(normed, pw[2]).astype(BF16)
    spread_out(gate, send_g)
    recv_g[me] = send_g[me]
    a2a(send_g, recv_g, 1)
    for copy in t_y:
        copy.start()

    for copy in q_z:
        copy.wait_recv()
    for k in range(NZ):
        a_re[pl.ds(2 * k, 2), :] = qz[k, :, pl.ds(0, 128)]
    rows = []
    for block in range(QW // 128):
        for k in range(NZ):
            a_re[pl.ds(16 * block + 2 * k, 2), :] = qz[k, :, pl.ds(128 * block, 128)]
        rows.append(a_re[pl.ds(16 * block, 16), :].astype(BF16))
    qx[x] = jnp.concatenate(rows, axis=1)
    q_x = [q_copy(qx.at[x], qx.at[x], 8 + k, (d, z, lax.rem(x + k, NX), y)) for k in range(1, NX)]
    for copy in q_x:
        copy.start()

    loads[3].wait()
    for half in range(2):
        padded = dot(spread_ref[...], ow[pl.ds(384 * half, 384), :])
        wpad[pl.ds(512 * half, 512), :] = padded.astype(BF16)
    loads[4].wait()
    for part in range(2):
        for e in range(CH):
            filt_t[part, :, pl.ds(128 * e, 128)] = filt[part, e].T
    start_hi = start_ref[...] >> 7
    start_lo = start_ref[...] & 127
    end_hi = end_ref[...] >> 7
    end_lo = end_ref[...] & 127
    inside = jnp.where((row_id >= start_hi) & (row_id < end_hi), 1.0, 0.0)
    at_end = jnp.where(row_id == end_hi, 1.0, 0.0)
    at_start = jnp.where(row_id == start_hi, 1.0, 0.0)
    spans = jnp.concatenate([inside, at_end, at_start], axis=1).astype(BF16)

    for copy in t_y:
        copy.wait_recv()
    p1[...] = ((ry[0] + ry[1]) + (ry[2] + ry[3])).reshape(NX, NZ, D)
    rx[x] = p1[x]
    t_x = [t_copy(p1.at[lax.rem(x + k, NX)], rx.at[x], 4 + k, (d, z, lax.rem(x + k, NX), y)) for k in range(1, NX)]
    for copy in t_x:
        copy.start()
    for copy in q_x:
        copy.wait_recv()
    qf[d, y] = qx[...]
    q_y = [q_copy(qx, qf.at[d, y], 12 + k, (d, z, x, lax.rem(y + k, NY))) for k in range(1, NY)]
    for copy in q_y:
        copy.start()

    a2a_all(send_s, recv_s, 0).wait_recv()
    got = recv_s[...].astype(F32).reshape(1024, 128).astype(BF16)
    spec = dot(jnp.concatenate([got, got], axis=1), f1_ref[...])
    spec_re = spec[:, :128].reshape(128, 8, 128)
    spec_im = spec[:, 128:].reshape(128, 8, 128)
    cos_x, sin_x = twx_ref[0], twx_ref[1]
    a_re[pl.ds(0, 1024), :] = (spec_re * cos_x + spec_im * sin_x).reshape(1024, 128)
    a_im[pl.ds(0, 1024), :] = (spec_im * cos_x - spec_re * sin_x).reshape(1024, 128)

    def columns(ref):
        return jnp.concatenate(
            [ref[pl.ds(e, 128, stride=8), :] for e in range(CH)], axis=1
        )

    def triple(left_ref, value):
        high, low = halves(value)
        return dot(left_ref[0], high) + (dot(left_ref[0], low) + dot(left_ref[1], high))

    full = triple(f2_ref, jnp.concatenate([columns(a_re), columns(a_im)], axis=0))
    full_re, full_im = full[:128], full[128:]
    h_re, h_im = filt_t[0], filt_t[1]
    prod = jnp.concatenate(
        [full_re * h_re - full_im * h_im, full_re * h_im + full_im * h_re], axis=0
    )
    back = triple(f3_ref, prod)
    back_re, back_im = back[:128], back[128:]
    cos_t, sin_t = tw_ref[0], tw_ref[1]
    turned = []
    for e in range(CH):
        e_re = back_re[:, 128 * e : 128 * (e + 1)]
        e_im = back_im[:, 128 * e : 128 * (e + 1)]
        turned.append(
            jnp.concatenate([e_re * cos_t - e_im * sin_t, e_re * sin_t + e_im * cos_t], axis=1)
        )
    high, low = halves(jnp.concatenate(turned, axis=0))
    conv = dot(high, f4_ref[0]) + (dot(low, f4_ref[0]) + dot(high, f4_ref[1]))
    for e in range(CH):
        conv_ref[pl.ds(e, 128, stride=8), :] = conv[128 * e : 128 * (e + 1)]
    for e in range(CH, 8):
        conv_ref[pl.ds(e, 128, stride=8), :] = jnp.zeros((128, 128), F32)

    a2a_all(send_g, recv_g, 1).wait_recv()
    gated = (recv_g[...].astype(F32) * conv_ref[pl.ds(0, 1024), :].reshape(128, 8, 128)).astype(BF16)
    gated_wide = gated.astype(F32).reshape(1024, 128)
    sums = dot(gated_wide.astype(BF16), spans)
    shard_id = lax.broadcasted_iota(jnp.int32, (128, 1, 128), 0)
    below_end = jnp.where(shard_id < end_lo.reshape(1, 1, 128), 1.0, 0.0)
    below_start = jnp.where(shard_id < start_lo.reshape(1, 1, 128), 1.0, 0.0)
    pooled_t = jnp.sum(
        sums[:, :128].reshape(128, 8, 128)
        + below_end * sums[:, 128:256].reshape(128, 8, 128)
        - below_start * sums[:, 256:].reshape(128, 8, 128),
        axis=0,
    )
    piece_0 = pooled_t.astype(BF16).astype(F32)
    rest = pooled_t - piece_0
    piece_1 = rest.astype(BF16).astype(F32)
    piece_2 = rest - piece_1
    pieces = jnp.concatenate(
        [piece_0, piece_1, piece_2, jnp.zeros((104, 128), F32)], axis=0
    ).T
    conv_ref[pl.ds(0, 1024), :] = gated_wide
    conv_ref[pl.ds(CH, 128, stride=8), :] = pieces
    send_2[...] = conv_ref[pl.ds(0, 1024), :].reshape(128, 8, 128).astype(BF16)
    recv_2[me] = send_2[me]
    a2a(send_2, recv_2, 2)

    for copy in t_x:
        copy.wait_recv()
    total_z = (rx[0] + rx[1]) + (rx[2] + rx[3])
    for k in range(NZ):
        p2[k] = total_z[k : k + 1]
    rz[z] = p2[z]
    t_z = [t_copy(p2.at[lax.rem(z + k, NZ)], rz.at[z], 8 + k, (d, lax.rem(z + k, NZ), x, y)) for k in range(1, NZ)]
    for copy in t_z:
        copy.start()
    for copy in q_y:
        copy.wait_recv()
    q_d = q_copy(qf.at[d], qf.at[d], 16, (1 - d, z, x, y))
    q_d.start()
    q_d.wait_recv()

    queries = qf[...].reshape(512, QW)
    wide_q = queries[:, :D].astype(F32)
    label_col = queries[:, D : D + 1].astype(F32)
    q_inv = lax.rsqrt(jnp.sum(wide_q * wide_q, axis=1, keepdims=True) + EPS)
    for copy in t_z:
        copy.wait_recv()
    token_sum = jnp.sum(rz[...], axis=0)
    mine = lax.broadcasted_iota(jnp.int32, (1, 128), 1) == me
    count = jnp.sum(jnp.where(mine, end_row - start_row, 0.0), axis=1, keepdims=True)

    a2a_all(send_2, recv_2, 2).wait_recv()
    back_rows = recv_2[...].astype(F32)
    row_in = lax.broadcasted_iota(jnp.int32, (1, 8, 128), 1)
    lane_in = lax.broadcasted_iota(jnp.int32, (1, 8, 128), 2)
    own_lane = ((lane_in & 7) == row_in) & (lane_in < 24)
    pool_rows = jnp.where(own_lane, back_rows[:, CH : CH + 1, :], 0.0)
    both = jnp.concatenate(
        [back_rows.reshape(1024, 128), pool_rows.reshape(1024, 128)], axis=1
    ).astype(BF16)
    mixed = lax.dot_general(
        both, wpad[...], (((0,), (0,)), ((), ())), preferred_element_type=F32
    )
    out_ref[...] = (mixed[:128] + wide).astype(BF16)

    pooled = (token_sum + jnp.sum(mixed[128:152], axis=0, keepdims=True)) / count
    inv = lax.rsqrt(jnp.sum(pooled * pooled, axis=1, keepdims=True) + EPS)
    unit = pooled * inv
    logits = SCALE * (jnp.sum(wide_q * unit, axis=1, keepdims=True) * q_inv) + OFFSET
    passage = (d * 128 + me).astype(F32)
    sign = jnp.where(label_col == passage, 1.0, -1.0)
    weight = -sign / (1.0 + jnp.exp(sign * logits))
    unit_grad = SCALE * jnp.sum((weight * q_inv) * wide_q, axis=0, keepdims=True)
    radial = jnp.sum(unit * unit_grad, axis=1, keepdims=True)
    grad_ref[...] = inv * (unit_grad - unit * radial)

    for src, dst, slot in ((send_s, recv_s, 0), (send_g, recv_g, 1), (send_2, recv_2, 2)):
        a2a_all(src, dst, slot).wait_send()
    for copy in q_z + q_x + q_y + [q_d] + t_y + t_x + t_z:
        copy.wait_send()


def per_device(
    tokens, norm_gain, proj_weight, out_weight, filter_spectrum,
    span_start, span_end, queries, labels,
):
    vmem = pl.BlockSpec(memory_space=pltpu.VMEM)
    hbm = pl.BlockSpec(memory_space=pl.ANY)
    smem = pl.BlockSpec(memory_space=pltpu.SMEM)
    consts = [jnp.asarray(table) for table in tables()]
    dma = pltpu.SemaphoreType.DMA
    slab = pltpu.VMEM((SHARDS, 8, 128), BF16)
    layer, grad = pl.pallas_call(
        kernel,
        name="layer",
        out_shape=(
            jax.ShapeDtypeStruct((TOK, D), BF16),
            jax.ShapeDtypeStruct((1, D), F32),
        ),
        in_specs=[vmem, vmem, hbm, hbm, hbm, vmem, vmem, vmem, smem] + [vmem] * 7,
        out_specs=(vmem, vmem),
        scratch_shapes=[
            pltpu.VMEM((3, D, D), BF16),
            pltpu.VMEM((D, D), BF16),
            pltpu.VMEM((2, CH, 128, 128), F32),
            pltpu.VMEM((1024, D), BF16),
            pltpu.VMEM((2, 128, D), F32),
            slab, slab, slab, slab, slab, slab,
            pltpu.VMEM((1032, 128), F32),
            pltpu.VMEM((1032, 128), F32),
            pltpu.VMEM((1032, 128), F32),
            pltpu.VMEM((NZ, 2, QW), F32),
            pltpu.VMEM((NX, 16, QW), BF16),
            pltpu.VMEM((2, NY, NX, 16, QW), BF16),
            pltpu.VMEM((NY, 32, D), F32),
            pltpu.VMEM((NY, 32, D), F32),
            pltpu.VMEM((NX, NZ, D), F32),
            pltpu.VMEM((NX, NZ, D), F32),
            pltpu.VMEM((NZ, 1, D), F32),
            pltpu.VMEM((NZ, 1, D), F32),
            dma((5,)), dma((3,)), dma((3,)), dma((17,)), dma((17,)), dma((16,)), dma((16,)),
        ],
        compiler_params=pltpu.CompilerParams(
            collective_id=0, has_side_effects=True, vmem_limit_bytes=48 * 2**20
        ),
    )(
        tokens.reshape(TOK, D), norm_gain.reshape(1, D), proj_weight, out_weight,
        filter_spectrum, span_start, span_end, queries, labels, *consts,
    )
    return layer.reshape(1, 1, TOK, D), grad.reshape(1, 1, D)


def solution(mesh):
    torus = Mesh(mesh.devices.reshape(mesh.shape["doc"], NZ, NX, NY), DOC_SEQ)
    placed = (
        P("doc", SEQ, None, None),
        P(),
        P(),
        P(),
        P(None, SEQ, None, None),
        P("doc", None),
        P("doc", None),
        P(DOC_SEQ, None),
        P(DOC_SEQ),
    )
    return jax.shard_map(
        per_device,
        mesh=torus,
        in_specs=placed,
        out_specs=(P("doc", SEQ, None, None), P("doc", SEQ, None)),
        check_vma=False,
    )
```

```python
import functools
import math

import jax
import jax.numpy as jnp
import ml_dtypes
import numpy as np
from jax import lax
from jax.experimental import pallas as pl
from jax.experimental.pallas import tpu as pltpu
from jax.sharding import Mesh
from jax.sharding import PartitionSpec as P

SEQ = ("seq_0", "seq_1", "seq_2")
DOC_SEQ = ("doc", "seq_0", "seq_1", "seq_2")
MESH = pl.DeviceIdType.MESH

NZ, NX, NY = 8, 4, 4
SHARDS = 128
TOK = 128
D = 768
CH = 6
N = TOK * SHARDS
QW = D + 128
EPS = 1e-06
SCALE = 10.0
OFFSET = -4.0
F32 = jnp.float32
BF16 = jnp.bfloat16


def split_table(table):
    high = table.astype(ml_dtypes.bfloat16)
    low = (table - high.astype(np.float64)).astype(ml_dtypes.bfloat16)
    return high, low


def tables():
    index = np.arange(128)
    angle = 2.0 * math.pi * ((index[:, None] * index[None, :]) % 128) / 128
    cosine, sine = np.cos(angle), np.sin(angle)
    first = np.stack(split_table(np.concatenate([cosine, -sine], axis=1)))
    first = first.reshape(256, 256)
    second = np.stack(split_table(np.block([[cosine, sine], [-sine, cosine]])))
    third = np.stack(split_table(np.block([[cosine, -sine], [sine, cosine]])))
    fourth = np.stack(split_table(np.concatenate([cosine, -sine], axis=0) / N))
    twist = 2.0 * math.pi * (index[:, None] * index[None, :]) / N
    twist = np.stack([np.cos(twist), np.sin(twist)]).astype(np.float32)
    spread = np.zeros((512, 384), np.float32)
    for slot in range(64):
        for row in range(CH):
            spread[8 * slot + row, CH * slot + row] = 1.0
    spread = spread.astype(ml_dtypes.bfloat16)
    return first, second, third, fourth, twist, twist[:, :, None, :], spread


def dot(a, b):
    return jnp.dot(a, b, preferred_element_type=F32)


def halves(value):
    high = value.astype(BF16)
    low = (value - high.astype(F32)).astype(BF16)
    return high, low


def kernel(
    tok_hbm, gain_hbm, pw_hbm, ow_hbm, filt_hbm, start_hbm, end_hbm, q_hbm, lab_hbm,
    f1_hbm, f2_hbm, f3_hbm, f4_hbm, tw_hbm, twx_hbm, spread_hbm,
    out_ref, grad_ref,
    tok_ref, gain_ref, start_ref, end_ref, q_ref, lab_ref,
    f1_ref, f2_ref, f3_ref, f4_ref, tw_ref, twx_ref, spread_ref,
    pw, ow, filt, wpad, filt_t,
    send_s, send_g, recv_s, recv_g, send_2, recv_2,
    a_re, a_im, conv_ref,
    qz, qx, qf,
    p0, ry, p1, rx, p2, rz,
    load_sem, a2a_send, a2a_recv, q_send, q_recv, t_send, t_recv,
):
    d = lax.axis_index("doc")
    z = lax.axis_index("seq_0")
    x = lax.axis_index("seq_1")
    y = lax.axis_index("seq_2")
    me = z * 16 + x * 4 + y

    pairs = [
        (tok_hbm, tok_ref), (gain_hbm, gain_ref.at[0]),
        (pw_hbm.at[:, pl.ds(0, D)], pw.at[0]), (pw_hbm.at[:, pl.ds(D, D)], pw.at[1]),
        (spread_hbm, spread_ref), (pw_hbm.at[:, pl.ds(2 * D, D)], pw.at[2]),
        (q_hbm, q_ref), (lab_hbm, lab_ref), (start_hbm, start_ref), (end_hbm, end_ref),
        (ow_hbm, ow), (filt_hbm, filt), (f1_hbm, f1_ref), (twx_hbm, twx_ref),
        (f2_hbm, f2_ref), (f3_hbm, f3_ref), (tw_hbm, tw_ref), (f4_hbm, f4_ref),
    ]
    loads = [
        pltpu.make_async_copy(src, dst, load_sem.at[slot])
        for slot, (src, dst) in enumerate(pairs)
    ]
    for load in loads[:6]:
        load.start()

    def arrived(*slots):
        for slot in slots:
            loads[slot].wait()

    ring_z = [lax.rem(z + k, NZ) for k in range(NZ)]
    ring_x = [lax.rem(x + k, NX) for k in range(NX)]
    ring_y = [lax.rem(y + k, NY) for k in range(NY)]

    def all_peers(visit):
        def plane(step, carry):
            kz = 4 + lax.div(step + 1, 2) * (1 - 2 * lax.rem(step, 2))
            pz = lax.rem(z + kz, NZ)
            for kx in (2, 1, 3, 0):
                for ky in (2, 1, 3, 0):
                    visit(pz, ring_x[kx], ring_y[ky])
            return carry

        lax.fori_loop(0, NZ - 1, plane, 0)
        for kx in (2, 1, 3, 0):
            for ky in (2, 1, 3, 0):
                if kx or ky:
                    visit(z, ring_x[kx], ring_y[ky])

    barrier = pltpu.get_barrier_semaphore()

    def greet(pz, px, py):
        pl.semaphore_signal(barrier, inc=1, device_id=(d, pz, px, py), device_id_type=MESH)

    all_peers(greet)
    pl.semaphore_signal(barrier, inc=1, device_id=(1 - d, z, x, y), device_id_type=MESH)

    for load in loads[6:]:
        load.start()

    arrived(0, 1)
    tokens = tok_ref[...]
    wide = tokens.astype(F32)
    rms = lax.rsqrt(jnp.mean(wide * wide, axis=1, keepdims=True) + EPS)
    normed = (wide * rms * gain_ref[...]).astype(BF16)

    def q_copy(src, dst, slot, dev):
        return pltpu.make_async_remote_copy(
            src_ref=src, dst_ref=dst, send_sem=q_send.at[slot], recv_sem=q_recv.at[slot],
            device_id=dev, device_id_type=MESH,
        )

    def t_copy(src, dst, slot, dev):
        return pltpu.make_async_remote_copy(
            src_ref=src, dst_ref=dst, send_sem=t_send.at[slot], recv_sem=t_recv.at[slot],
            device_id=dev, device_id_type=MESH,
        )

    arrived(2, 3, 4)
    signal = (dot(normed, pw[0]) * dot(normed, pw[1])).astype(BF16)
    contract = (((1,), (1,)), ((), ()))

    def spread_out(value, target):
        for half in range(2):
            part = lax.dot_general(
                spread_ref[...], value[:, 384 * half : 384 * (half + 1)], contract,
                preferred_element_type=F32,
            )
            target[pl.ds(64 * half, 64)] = part.reshape(64, 8, 128).astype(BF16)

    spread_out(signal, send_s)
    recv_s[me] = send_s[me]

    def a2a(src, dst, slot):
        def send(pz, px, py):
            pltpu.make_async_remote_copy(
                src_ref=src.at[pz * 16 + px * 4 + py], dst_ref=dst.at[me],
                send_sem=a2a_send.at[slot], recv_sem=a2a_recv.at[slot],
                device_id=(d, pz, px, py), device_id_type=MESH,
            ).start()

        all_peers(send)

    def a2a_all(src, dst, slot):
        return pltpu.make_async_remote_copy(
            src_ref=src.at[pl.ds(0, SHARDS - 1)], dst_ref=dst.at[pl.ds(0, SHARDS - 1)],
            send_sem=a2a_send.at[slot], recv_sem=a2a_recv.at[slot],
            device_id=(d, ring_z[1], x, y), device_id_type=MESH,
        )

    pl.semaphore_wait(barrier, SHARDS)
    a2a(send_s, recv_s, 0)
    arrived(6, 7, 8, 9)
    qz[z, :, pl.ds(0, D)] = q_ref[...].astype(F32)
    label_row = lax.broadcasted_iota(jnp.int32, (2, 128), 0)
    qz[z, :, pl.ds(D, 128)] = jnp.where(label_row == 0, lab_ref[0], lab_ref[1]).astype(F32)

    q_z = [q_copy(qz.at[z], qz.at[z], k, (d, ring_z[k], x, y)) for k in range(1, NZ)]
    for copy in q_z:
        copy.start()


    arrived(5)
    gate = dot(normed, pw[2]).astype(BF16)
    spread_out(gate, send_g)
    recv_g[me] = send_g[me]
    a2a(send_g, recv_g, 1)
    start_row = start_ref[...].astype(F32)
    end_row = end_ref[...].astype(F32)
    row_id = lax.broadcasted_iota(jnp.int32, (128, 128), 0)
    lane_id = lax.broadcasted_iota(jnp.int32, (128, 128), 1)
    wanted = ((row_id & 7) << 4) | (((row_id >> 3) & 3) << 2) | (row_id >> 5)
    pick = lane_id == wanted
    start_col = jnp.sum(jnp.where(pick, start_row, 0.0), axis=1, keepdims=True)
    end_col = jnp.sum(jnp.where(pick, end_row, 0.0), axis=1, keepdims=True)
    position = (lane_id * SHARDS + me).astype(F32)
    member = jnp.where((position >= start_col) & (position < end_col), 1.0, 0.0).astype(BF16)
    p0[...] = dot(member, tokens).reshape(NY, 32, D)
    ry[y] = p0[y]

    t_y = [t_copy(p0.at[ring_y[k]], ry.at[y], k, (d, z, x, ring_y[k])) for k in range(1, NY)]
    for copy in t_y:
        copy.start()

    arrived(10)
    for half in range(2):
        padded = dot(spread_ref[...], ow[pl.ds(384 * half, 384), :])
        wpad[pl.ds(512 * half, 512), :] = padded.astype(BF16)
    arrived(11)
    for part in range(2):
        for e in range(CH):
            filt_t[part, :, pl.ds(128 * e, 128)] = filt[part, e].T
    start_hi = start_ref[...] >> 7
    start_lo = start_ref[...] & 127
    end_hi = end_ref[...] >> 7
    end_lo = end_ref[...] & 127
    inside = jnp.where((row_id >= start_hi) & (row_id < end_hi), 1.0, 0.0)
    at_end = jnp.where(row_id == end_hi, 1.0, 0.0)
    at_start = jnp.where(row_id == start_hi, 1.0, 0.0)
    spans = jnp.concatenate([inside, at_end, at_start], axis=1).astype(BF16)

    for copy in q_z:
        copy.wait_recv()
    for k in range(NZ):
        a_re[pl.ds(2 * k, 2), :] = qz[k, :, pl.ds(0, 128)]
    rows = []
    for block in range(QW // 128):
        for k in range(NZ):
            a_re[pl.ds(16 * block + 2 * k, 2), :] = qz[k, :, pl.ds(128 * block, 128)]
        rows.append(a_re[pl.ds(16 * block, 16), :].astype(BF16))
    qx[x] = jnp.concatenate(rows, axis=1)
    q_x = [q_copy(qx.at[x], qx.at[x], 8 + k, (d, z, ring_x[k], y)) for k in range(1, NX)]
    for copy in q_x:
        copy.start()

    arrived(12, 13, 14, 15, 16, 17)
    a2a_all(send_s, recv_s, 0).wait_recv()
    got = recv_s[...].astype(F32).reshape(1024, 128).astype(BF16)
    spec = dot(jnp.concatenate([got, got], axis=1), f1_ref[...])
    spec_re = spec[:, :128].reshape(128, 8, 128)
    spec_im = spec[:, 128:].reshape(128, 8, 128)
    cos_x, sin_x = twx_ref[0], twx_ref[1]
    a_re[pl.ds(0, 1024), :] = (spec_re * cos_x + spec_im * sin_x).reshape(1024, 128)
    a_im[pl.ds(0, 1024), :] = (spec_im * cos_x - spec_re * sin_x).reshape(1024, 128)

    def columns(ref):
        return jnp.concatenate(
            [ref[pl.ds(e, 128, stride=8), :] for e in range(CH)], axis=1
        )

    def triple(left_ref, value):
        high, low = halves(value)
        return dot(left_ref[0], high) + (dot(left_ref[0], low) + dot(left_ref[1], high))

    full = triple(f2_ref, jnp.concatenate([columns(a_re), columns(a_im)], axis=0))
    full_re, full_im = full[:128], full[128:]
    h_re, h_im = filt_t[0], filt_t[1]
    prod = jnp.concatenate(
        [full_re * h_re - full_im * h_im, full_re * h_im + full_im * h_re], axis=0
    )
    back = triple(f3_ref, prod)
    back_re, back_im = back[:128], back[128:]
    cos_t, sin_t = tw_ref[0], tw_ref[1]
    turned = []
    for e in range(CH):
        e_re = back_re[:, 128 * e : 128 * (e + 1)]
        e_im = back_im[:, 128 * e : 128 * (e + 1)]
        turned.append(
            jnp.concatenate([e_re * cos_t - e_im * sin_t, e_re * sin_t + e_im * cos_t], axis=1)
        )
    high, low = halves(jnp.concatenate(turned, axis=0))
    conv = dot(high, f4_ref[0]) + (dot(low, f4_ref[0]) + dot(high, f4_ref[1]))
    for e in range(CH):
        conv_ref[pl.ds(e, 128, stride=8), :] = conv[128 * e : 128 * (e + 1)]
    for e in range(CH, 8):
        conv_ref[pl.ds(e, 128, stride=8), :] = jnp.zeros((128, 128), F32)

    for copy in q_x:
        copy.wait_recv()
    qf[d, y] = qx[...]
    q_y = [q_copy(qx, qf.at[d, y], 12 + k, (d, z, x, ring_y[k])) for k in range(1, NY)]
    for copy in q_y:
        copy.start()

    for copy in t_y:
        copy.wait_recv()
    p1[...] = ((ry[0] + ry[1]) + (ry[2] + ry[3])).reshape(NX, NZ, D)
    rx[x] = p1[x]
    t_x = [t_copy(p1.at[ring_x[k]], rx.at[x], 4 + k, (d, z, ring_x[k], y)) for k in range(1, NX)]
    for copy in t_x:
        copy.start()
    a2a_all(send_g, recv_g, 1).wait_recv()
    gated = (recv_g[...].astype(F32) * conv_ref[pl.ds(0, 1024), :].reshape(128, 8, 128)).astype(BF16)
    gated_wide = gated.astype(F32).reshape(1024, 128)
    sums = dot(gated_wide.astype(BF16), spans)
    shard_id = lax.broadcasted_iota(jnp.int32, (128, 1, 128), 0)
    below_end = jnp.where(shard_id < end_lo.reshape(1, 1, 128), 1.0, 0.0)
    below_start = jnp.where(shard_id < start_lo.reshape(1, 1, 128), 1.0, 0.0)
    pooled_t = jnp.sum(
        sums[:, :128].reshape(128, 8, 128)
        + below_end * sums[:, 128:256].reshape(128, 8, 128)
        - below_start * sums[:, 256:].reshape(128, 8, 128),
        axis=0,
    )
    piece_0 = pooled_t.astype(BF16).astype(F32)
    rest = pooled_t - piece_0
    piece_1 = rest.astype(BF16).astype(F32)
    piece_2 = rest - piece_1
    pieces = jnp.concatenate(
        [piece_0, piece_1, piece_2, jnp.zeros((104, 128), F32)], axis=0
    ).T
    conv_ref[pl.ds(0, 1024), :] = gated_wide
    conv_ref[pl.ds(CH, 128, stride=8), :] = pieces
    send_2[...] = conv_ref[pl.ds(0, 1024), :].reshape(128, 8, 128).astype(BF16)
    recv_2[me] = send_2[me]
    a2a(send_2, recv_2, 2)

    for copy in t_x:
        copy.wait_recv()
    total_z = (rx[0] + rx[1]) + (rx[2] + rx[3])
    for k in range(NZ):
        p2[k] = total_z[k : k + 1]
    rz[z] = p2[z]
    t_z = [t_copy(p2.at[ring_z[k]], rz.at[z], 8 + k, (d, ring_z[k], x, y)) for k in range(1, NZ)]
    for copy in t_z:
        copy.start()
    for copy in q_y:
        copy.wait_recv()
    q_d = q_copy(qf.at[d], qf.at[d], 16, (1 - d, z, x, y))
    q_d.start()
    q_d.wait_recv()

    queries = qf[...].reshape(512, QW)
    wide_q = queries[:, :D].astype(F32)
    label_col = queries[:, D : D + 1].astype(F32)
    q_inv = lax.rsqrt(jnp.sum(wide_q * wide_q, axis=1, keepdims=True) + EPS)
    for copy in t_z:
        copy.wait_recv()
    token_sum = jnp.sum(rz[...], axis=0)
    mine = lax.broadcasted_iota(jnp.int32, (1, 128), 1) == me
    count = jnp.sum(jnp.where(mine, end_row - start_row, 0.0), axis=1, keepdims=True)

    a2a_all(send_2, recv_2, 2).wait_recv()
    back_rows = recv_2[...].astype(F32)
    row_in = lax.broadcasted_iota(jnp.int32, (1, 8, 128), 1)
    lane_in = lax.broadcasted_iota(jnp.int32, (1, 8, 128), 2)
    own_lane = ((lane_in & 7) == row_in) & (lane_in < 24)
    pool_rows = jnp.where(own_lane, back_rows[:, CH : CH + 1, :], 0.0)
    both = jnp.concatenate(
        [back_rows.reshape(1024, 128), pool_rows.reshape(1024, 128)], axis=1
    ).astype(BF16)
    mixed = lax.dot_general(
        both, wpad[...], (((0,), (0,)), ((), ())), preferred_element_type=F32
    )
    out_ref[...] = (mixed[:128] + wide).astype(BF16)

    pooled = (token_sum + jnp.sum(mixed[128:152], axis=0, keepdims=True)) / count
    inv = lax.rsqrt(jnp.sum(pooled * pooled, axis=1, keepdims=True) + EPS)
    unit = pooled * inv
    logits = SCALE * (jnp.sum(wide_q * unit, axis=1, keepdims=True) * q_inv) + OFFSET
    passage = (d * 128 + me).astype(F32)
    sign = jnp.where(label_col == passage, 1.0, -1.0)
    weight = -sign / (1.0 + jnp.exp(sign * logits))
    unit_grad = SCALE * jnp.sum((weight * q_inv) * wide_q, axis=0, keepdims=True)
    radial = jnp.sum(unit * unit_grad, axis=1, keepdims=True)
    grad_ref[...] = inv * (unit_grad - unit * radial)

    for src, dst, slot in ((send_s, recv_s, 0), (send_g, recv_g, 1), (send_2, recv_2, 2)):
        a2a_all(src, dst, slot).wait_send()
    for copy in q_z + q_x + q_y + [q_d] + t_y + t_x + t_z:
        copy.wait_send()


def per_device(
    tokens, norm_gain, proj_weight, out_weight, filter_spectrum,
    span_start, span_end, queries, labels,
):
    vmem = pl.BlockSpec(memory_space=pltpu.VMEM)
    hbm = pl.BlockSpec(memory_space=pl.ANY)
    consts = [jnp.asarray(table) for table in tables()]
    dma = pltpu.SemaphoreType.DMA
    slab = pltpu.VMEM((SHARDS, 8, 128), BF16)
    layer, grad = pl.pallas_call(
        kernel,
        name="layer",
        out_shape=(
            pltpu.VMEM((TOK, D), BF16),
            pltpu.VMEM((1, D), F32),
        ),
        in_specs=[hbm] * 16,
        out_specs=(vmem, vmem),
        scratch_shapes=[
            pltpu.VMEM((TOK, D), BF16),
            pltpu.VMEM((1, D), F32),
            pltpu.VMEM((1, SHARDS), jnp.int32),
            pltpu.VMEM((1, SHARDS), jnp.int32),
            pltpu.VMEM((2, D), BF16),
            pltpu.SMEM((2,), jnp.int32),
            *[pltpu.VMEM(table.shape, table.dtype) for table in consts],
            pltpu.VMEM((3, D, D), BF16),
            pltpu.VMEM((D, D), BF16),
            pltpu.VMEM((2, CH, 128, 128), F32),
            pltpu.VMEM((1024, D), BF16),
            pltpu.VMEM((2, 128, D), F32),
            slab, slab, slab, slab, slab, slab,
            pltpu.VMEM((1032, 128), F32),
            pltpu.VMEM((1032, 128), F32),
            pltpu.VMEM((1032, 128), F32),
            pltpu.VMEM((NZ, 2, QW), F32),
            pltpu.VMEM((NX, 16, QW), BF16),
            pltpu.VMEM((2, NY, NX, 16, QW), BF16),
            pltpu.VMEM((NY, 32, D), F32),
            pltpu.VMEM((NY, 32, D), F32),
            pltpu.VMEM((NX, NZ, D), F32),
            pltpu.VMEM((NX, NZ, D), F32),
            pltpu.VMEM((NZ, 1, D), F32),
            pltpu.VMEM((NZ, 1, D), F32),
            dma((18,)), dma((3,)), dma((3,)), dma((17,)), dma((17,)), dma((16,)), dma((16,)),
        ],
        compiler_params=pltpu.CompilerParams(
            collective_id=0, has_side_effects=True, vmem_limit_bytes=63 * 2**20
        ),
    )(
        tokens.reshape(TOK, D), norm_gain, proj_weight, out_weight,
        filter_spectrum, span_start, span_end, queries, labels, *consts,
    )
    return layer.reshape(1, 1, TOK, D), grad.reshape(1, 1, D)


def solution(mesh):
    torus = Mesh(mesh.devices.reshape(mesh.shape["doc"], NZ, NX, NY), DOC_SEQ)
    placed = (
        P("doc", SEQ, None, None),
        P(),
        P(),
        P(),
        P(None, SEQ, None, None),
        P("doc", None),
        P("doc", None),
        P(DOC_SEQ, None),
        P(DOC_SEQ),
    )
    return jax.shard_map(
        per_device,
        mesh=torus,
        in_specs=placed,
        out_specs=(P("doc", SEQ, None, None), P("doc", SEQ, None)),
        check_vma=False,
    )
```

```python
import functools
import math

import jax
import jax.numpy as jnp
import ml_dtypes
import numpy as np
from jax import lax
from jax.experimental import pallas as pl
from jax.experimental.pallas import tpu as pltpu
from jax.sharding import Mesh
from jax.sharding import PartitionSpec as P

SEQ = ("seq_0", "seq_1", "seq_2")
DOC_SEQ = ("doc", "seq_0", "seq_1", "seq_2")
MESH = pl.DeviceIdType.MESH

NZ, NX, NY = 8, 4, 4
SHARDS = 128
TOK = 128
D = 768
CH = 6
N = TOK * SHARDS
QW = D + 128
EPS = 1e-06
SCALE = 10.0
OFFSET = -4.0
F32 = jnp.float32
BF16 = jnp.bfloat16


def split_table(table):
    high = table.astype(ml_dtypes.bfloat16)
    low = (table - high.astype(np.float64)).astype(ml_dtypes.bfloat16)
    return high, low


def tables():
    index = np.arange(128)
    angle = 2.0 * math.pi * ((index[:, None] * index[None, :]) % 128) / 128
    cosine, sine = np.cos(angle), np.sin(angle)
    first = np.stack(split_table(np.concatenate([cosine, -sine], axis=1)))
    first = first.reshape(256, 256)
    second = np.stack(split_table(np.block([[cosine, sine], [-sine, cosine]])))
    third = np.stack(split_table(np.block([[cosine, -sine], [sine, cosine]])))
    fourth = np.stack(split_table(np.concatenate([cosine, -sine], axis=0) / N))
    twist = 2.0 * math.pi * (index[:, None] * index[None, :]) / N
    twist = np.stack([np.cos(twist), np.sin(twist)]).astype(np.float32)
    spread = np.zeros((512, 384), np.float32)
    for slot in range(64):
        for row in range(CH):
            spread[8 * slot + row, CH * slot + row] = 1.0
    spread = spread.astype(ml_dtypes.bfloat16)
    return first, second, third, fourth, twist, twist[:, :, None, :], spread


def dot(a, b):
    return jnp.dot(a, b, preferred_element_type=F32)


def halves(value):
    high = value.astype(BF16)
    low = (value - high.astype(F32)).astype(BF16)
    return high, low


def kernel(
    tok_hbm, gain_hbm, pw_hbm, ow_hbm, filt_hbm, start_hbm, end_hbm, q_hbm, lab_hbm,
    f1_hbm, f2_hbm, f3_hbm, f4_hbm, tw_hbm, twx_hbm, spread_hbm,
    out_ref, grad_ref,
    tok_ref, gain_ref, start_ref, end_ref, q_ref, lab_ref,
    f1_ref, f2_ref, f3_ref, f4_ref, tw_ref, twx_ref, spread_ref,
    pw, ow, filt, wpad, filt_t,
    send_s, send_g, recv_s, recv_g, send_2, recv_2,
    a_re, a_im, conv_ref, pool_ref,
    qz, qx, qf,
    p0, ry, p1, rx, p2, rz,
    load_sem, a2a_send, a2a_recv, q_send, q_recv, t_send, t_recv,
):
    d = lax.axis_index("doc")
    z = lax.axis_index("seq_0")
    x = lax.axis_index("seq_1")
    y = lax.axis_index("seq_2")
    me = z * 16 + x * 4 + y

    pairs = [
        (tok_hbm, tok_ref), (gain_hbm, gain_ref.at[0]),
        (pw_hbm.at[:, pl.ds(0, D)], pw.at[0]), (pw_hbm.at[:, pl.ds(D, D)], pw.at[1]),
        (spread_hbm, spread_ref), (pw_hbm.at[:, pl.ds(2 * D, D)], pw.at[2]),
        (q_hbm, q_ref), (lab_hbm, lab_ref), (start_hbm, start_ref), (end_hbm, end_ref),
        (ow_hbm, ow), (filt_hbm, filt), (f1_hbm, f1_ref), (twx_hbm, twx_ref),
        (f2_hbm, f2_ref), (f3_hbm, f3_ref), (tw_hbm, tw_ref), (f4_hbm, f4_ref),
    ]
    loads = [
        pltpu.make_async_copy(src, dst, load_sem.at[slot])
        for slot, (src, dst) in enumerate(pairs)
    ]
    for load in loads[:6]:
        load.start()

    def arrived(*slots):
        for slot in slots:
            loads[slot].wait()

    ring_z = [lax.rem(z + k, NZ) for k in range(NZ)]
    ring_x = [lax.rem(x + k, NX) for k in range(NX)]
    ring_y = [lax.rem(y + k, NY) for k in range(NY)]

    def all_peers(visit):
        def plane(step, carry):
            kz = 4 + lax.div(step + 1, 2) * (1 - 2 * lax.rem(step, 2))
            pz = lax.rem(z + kz, NZ)
            for kx in (2, 1, 3, 0):
                for ky in (2, 1, 3, 0):
                    visit(pz, ring_x[kx], ring_y[ky])
            return carry

        lax.fori_loop(0, NZ - 1, plane, 0)
        for kx in (2, 1, 3, 0):
            for ky in (2, 1, 3, 0):
                if kx or ky:
                    visit(z, ring_x[kx], ring_y[ky])

    barrier = pltpu.get_barrier_semaphore()

    def greet(pz, px, py):
        pl.semaphore_signal(barrier, inc=1, device_id=(d, pz, px, py), device_id_type=MESH)

    all_peers(greet)
    pl.semaphore_signal(barrier, inc=1, device_id=(1 - d, z, x, y), device_id_type=MESH)

    for load in loads[6:]:
        load.start()

    arrived(0, 1)
    tokens = tok_ref[...]
    wide = tokens.astype(F32)
    rms = lax.rsqrt(jnp.mean(wide * wide, axis=1, keepdims=True) + EPS)
    normed = (wide * rms * gain_ref[...]).astype(BF16)

    def q_copy(src, dst, slot, dev):
        return pltpu.make_async_remote_copy(
            src_ref=src, dst_ref=dst, send_sem=q_send.at[slot], recv_sem=q_recv.at[slot],
            device_id=dev, device_id_type=MESH,
        )

    def t_copy(src, dst, slot, dev):
        return pltpu.make_async_remote_copy(
            src_ref=src, dst_ref=dst, send_sem=t_send.at[slot], recv_sem=t_recv.at[slot],
            device_id=dev, device_id_type=MESH,
        )

    arrived(2, 3, 4)
    signal = (dot(normed, pw[0]) * dot(normed, pw[1])).astype(BF16)
    contract = (((1,), (1,)), ((), ()))

    def spread_out(value, target):
        for half in range(2):
            part = lax.dot_general(
                spread_ref[...], value[:, 384 * half : 384 * (half + 1)], contract,
                preferred_element_type=F32,
            )
            target[pl.ds(64 * half, 64)] = part.reshape(64, 8, 128).astype(BF16)

    spread_out(signal, send_s)
    recv_s[me] = send_s[me]

    def a2a(src, dst, slot):
        def send(pz, px, py):
            pltpu.make_async_remote_copy(
                src_ref=src.at[pz * 16 + px * 4 + py], dst_ref=dst.at[me],
                send_sem=a2a_send.at[slot], recv_sem=a2a_recv.at[slot],
                device_id=(d, pz, px, py), device_id_type=MESH,
            ).start()

        all_peers(send)

    def a2a_all(src, dst, slot):
        return pltpu.make_async_remote_copy(
            src_ref=src.at[pl.ds(0, SHARDS - 1)], dst_ref=dst.at[pl.ds(0, SHARDS - 1)],
            send_sem=a2a_send.at[slot], recv_sem=a2a_recv.at[slot],
            device_id=(d, ring_z[1], x, y), device_id_type=MESH,
        )

    arrived(5)
    gate = dot(normed, pw[2]).astype(BF16)
    spread_out(gate, send_g)
    recv_g[me] = send_g[me]

    arrived(6, 7, 8, 9)
    start_row = start_ref[...].astype(F32)
    end_row = end_ref[...].astype(F32)
    row_id = lax.broadcasted_iota(jnp.int32, (128, 128), 0)
    lane_id = lax.broadcasted_iota(jnp.int32, (128, 128), 1)
    wanted = ((row_id & 7) << 4) | (((row_id >> 3) & 3) << 2) | (row_id >> 5)
    pick = lane_id == wanted
    start_col = jnp.sum(jnp.where(pick, start_row, 0.0), axis=1, keepdims=True)
    end_col = jnp.sum(jnp.where(pick, end_row, 0.0), axis=1, keepdims=True)
    position = (lane_id * SHARDS + me).astype(F32)
    member = jnp.where((position >= start_col) & (position < end_col), 1.0, 0.0).astype(BF16)
    p0[...] = dot(member, tokens).reshape(NY, 32, D)
    ry[y] = p0[y]

    qz[z, :, pl.ds(0, D)] = q_ref[...]
    label_row = lax.broadcasted_iota(jnp.int32, (2, 128), 0)
    qz[z, :, pl.ds(D, 128)] = jnp.where(label_row == 0, lab_ref[0], lab_ref[1]).astype(F32).astype(BF16)

    pl.semaphore_wait(barrier, SHARDS)
    q_z = [q_copy(qz.at[z], qz.at[z], k, (d, ring_z[k], x, y)) for k in range(1, NZ)]
    for copy in q_z:
        copy.start()
    t_y = [t_copy(p0.at[ring_y[k]], ry.at[y], k, (d, z, x, ring_y[k])) for k in range(1, NY)]
    for copy in t_y:
        copy.start()

    a2a(send_s, recv_s, 0)
    a2a(send_g, recv_g, 1)
    arrived(10)
    for half in range(2):
        padded = dot(spread_ref[...], ow[pl.ds(384 * half, 384), :])
        wpad[pl.ds(512 * half, 512), :] = padded.astype(BF16)
    arrived(11)
    for part in range(2):
        for e in range(CH):
            filt_t[part, :, pl.ds(128 * e, 128)] = filt[part, e].T
    for e in range(CH, 8):
        conv_ref[pl.ds(e, 128, stride=8), :] = jnp.zeros((128, 128), F32)
    pool_ref[...] = jnp.zeros_like(pool_ref)
    start_hi = start_ref[...] >> 7
    start_lo = start_ref[...] & 127
    end_hi = end_ref[...] >> 7
    end_lo = end_ref[...] & 127
    inside = jnp.where((row_id >= start_hi) & (row_id < end_hi), 1.0, 0.0)
    at_end = jnp.where(row_id == end_hi, 1.0, 0.0)
    at_start = jnp.where(row_id == start_hi, 1.0, 0.0)
    spans = jnp.concatenate([inside, at_end, at_start], axis=1).astype(BF16)

    for copy in q_z:
        copy.wait_recv()
    rows = []
    for block in range(QW // 128):
        for k in range(NZ):
            a_re[pl.ds(16 * block + 2 * k, 2), :] = qz[k, :, pl.ds(128 * block, 128)].astype(F32)
        rows.append(a_re[pl.ds(16 * block, 16), :].astype(BF16))
    qx[x] = jnp.concatenate(rows, axis=1)
    q_x = [q_copy(qx.at[x], qx.at[x], 8 + k, (d, z, ring_x[k], y)) for k in range(1, NX)]
    for copy in q_x:
        copy.start()

    for copy in t_y:
        copy.wait_recv()
    p1[...] = ((ry[0] + ry[1]) + (ry[2] + ry[3])).reshape(NX, NZ, D)
    rx[x] = p1[x]
    t_x = [t_copy(p1.at[ring_x[k]], rx.at[x], 4 + k, (d, z, ring_x[k], y)) for k in range(1, NX)]
    for copy in t_x:
        copy.start()

    arrived(12, 13, 14, 15, 16, 17)
    a2a_all(send_s, recv_s, 0).wait_recv()
    got = recv_s[...].astype(F32).reshape(1024, 128).astype(BF16)
    spec = dot(jnp.concatenate([got, got], axis=1), f1_ref[...])
    spec_re = spec[:, :128].reshape(128, 8, 128)
    spec_im = spec[:, 128:].reshape(128, 8, 128)
    cos_x, sin_x = twx_ref[0], twx_ref[1]
    a_re[pl.ds(0, 1024), :] = (spec_re * cos_x + spec_im * sin_x).reshape(1024, 128)
    a_im[pl.ds(0, 1024), :] = (spec_im * cos_x - spec_re * sin_x).reshape(1024, 128)

    def columns(ref):
        return jnp.concatenate(
            [ref[pl.ds(e, 128, stride=8), :] for e in range(CH)], axis=1
        )

    def triple(left_ref, value):
        high, low = halves(value)
        return dot(left_ref[0], high) + (dot(left_ref[0], low) + dot(left_ref[1], high))

    full = triple(f2_ref, jnp.concatenate([columns(a_re), columns(a_im)], axis=0))
    full_re, full_im = full[:128], full[128:]
    h_re, h_im = filt_t[0], filt_t[1]
    prod = jnp.concatenate(
        [full_re * h_re - full_im * h_im, full_re * h_im + full_im * h_re], axis=0
    )
    back = triple(f3_ref, prod)
    back_re, back_im = back[:128], back[128:]
    cos_t, sin_t = tw_ref[0], tw_ref[1]
    turned = []
    for e in range(CH):
        e_re = back_re[:, 128 * e : 128 * (e + 1)]
        e_im = back_im[:, 128 * e : 128 * (e + 1)]
        turned.append(
            jnp.concatenate([e_re * cos_t - e_im * sin_t, e_re * sin_t + e_im * cos_t], axis=1)
        )
    high, low = halves(jnp.concatenate(turned, axis=0))
    conv = dot(high, f4_ref[0]) + (dot(low, f4_ref[0]) + dot(high, f4_ref[1]))
    for e in range(CH):
        conv_ref[pl.ds(e, 128, stride=8), :] = conv[128 * e : 128 * (e + 1)]

    for copy in q_x:
        copy.wait_recv()
    qf[d, y] = qx[...]
    q_y = [q_copy(qx, qf.at[d, y], 12 + k, (d, z, x, ring_y[k])) for k in range(1, NY)]
    for copy in q_y:
        copy.start()

    for copy in t_x:
        copy.wait_recv()
    total_z = (rx[0] + rx[1]) + (rx[2] + rx[3])
    for k in range(NZ):
        p2[k] = total_z[k : k + 1]
    rz[z] = p2[z]
    t_z = [t_copy(p2.at[ring_z[k]], rz.at[z], 8 + k, (d, ring_z[k], x, y)) for k in range(1, NZ)]
    for copy in t_z:
        copy.start()

    a2a_all(send_g, recv_g, 1).wait_recv()
    gated = (recv_g[...].astype(F32) * conv_ref[pl.ds(0, 1024), :].reshape(128, 8, 128)).astype(BF16)
    gated_wide = gated.astype(F32).reshape(1024, 128)
    sums = dot(gated_wide.astype(BF16), spans)
    shard_id = lax.broadcasted_iota(jnp.int32, (128, 1, 128), 0)
    below_end = jnp.where(shard_id < end_lo.reshape(1, 1, 128), 1.0, 0.0)
    below_start = jnp.where(shard_id < start_lo.reshape(1, 1, 128), 1.0, 0.0)
    pooled_t = jnp.sum(
        sums[:, :128].reshape(128, 8, 128)
        + below_end * sums[:, 128:256].reshape(128, 8, 128)
        - below_start * sums[:, 256:].reshape(128, 8, 128),
        axis=0,
    )
    piece_0 = pooled_t.astype(BF16).astype(F32)
    rest = pooled_t - piece_0
    piece_1 = rest.astype(BF16).astype(F32)
    piece_2 = rest - piece_1
    pieces = jnp.concatenate(
        [piece_0, piece_1, piece_2, jnp.zeros((104, 128), F32)], axis=0
    ).T
    pool_ref[pl.ds(CH, 128, stride=8), :] = pieces
    send_2[...] = (gated_wide + pool_ref[pl.ds(0, 1024), :]).reshape(128, 8, 128).astype(BF16)
    recv_2[me] = send_2[me]
    a2a(send_2, recv_2, 2)

    for copy in q_y:
        copy.wait_recv()
    q_d = q_copy(qf.at[d], qf.at[d], 16, (1 - d, z, x, y))
    q_d.start()
    q_d.wait_recv()

    queries = qf[...].reshape(512, QW)
    wide_q = queries[:, :D].astype(F32)
    label_col = queries[:, D : D + 1].astype(F32)
    q_inv = lax.rsqrt(jnp.sum(wide_q * wide_q, axis=1, keepdims=True) + EPS)
    for copy in t_z:
        copy.wait_recv()
    token_sum = jnp.sum(rz[...], axis=0)
    mine = lax.broadcasted_iota(jnp.int32, (1, 128), 1) == me
    count = jnp.sum(jnp.where(mine, end_row - start_row, 0.0), axis=1, keepdims=True)

    a2a_all(send_2, recv_2, 2).wait_recv()
    back_rows = recv_2[...].astype(F32)
    row_in = lax.broadcasted_iota(jnp.int32, (1, 8, 128), 1)
    lane_in = lax.broadcasted_iota(jnp.int32, (1, 8, 128), 2)
    own_lane = ((lane_in & 7) == row_in) & (lane_in < 24)
    pool_rows = jnp.where(own_lane, back_rows[:, CH : CH + 1, :], 0.0)
    both = jnp.concatenate(
        [back_rows.reshape(1024, 128), pool_rows.reshape(1024, 128)], axis=1
    ).astype(BF16)
    mixed = lax.dot_general(
        both, wpad[...], (((0,), (0,)), ((), ())), preferred_element_type=F32
    )
    out_ref[...] = (mixed[:128] + wide).astype(BF16)

    pooled = (token_sum + jnp.sum(mixed[128:152], axis=0, keepdims=True)) / count
    inv = lax.rsqrt(jnp.sum(pooled * pooled, axis=1, keepdims=True) + EPS)
    unit = pooled * inv
    logits = SCALE * (jnp.sum(wide_q * unit, axis=1, keepdims=True) * q_inv) + OFFSET
    passage = (d * 128 + me).astype(F32)
    sign = jnp.where(label_col == passage, 1.0, -1.0)
    weight = -sign / (1.0 + jnp.exp(sign * logits))
    unit_grad = SCALE * jnp.sum((weight * q_inv) * wide_q, axis=0, keepdims=True)
    radial = jnp.sum(unit * unit_grad, axis=1, keepdims=True)
    grad_ref[...] = inv * (unit_grad - unit * radial)

    for src, dst, slot in ((send_s, recv_s, 0), (send_g, recv_g, 1), (send_2, recv_2, 2)):
        a2a_all(src, dst, slot).wait_send()
    for copy in q_z + q_x + q_y + [q_d] + t_y + t_x + t_z:
        copy.wait_send()


def per_device(
    tokens, norm_gain, proj_weight, out_weight, filter_spectrum,
    span_start, span_end, queries, labels,
):
    vmem = pl.BlockSpec(memory_space=pltpu.VMEM)
    hbm = pl.BlockSpec(memory_space=pl.ANY)
    consts = [jnp.asarray(table) for table in tables()]
    dma = pltpu.SemaphoreType.DMA
    slab = pltpu.VMEM((SHARDS, 8, 128), BF16)
    layer, grad = pl.pallas_call(
        kernel,
        name="layer",
        out_shape=(
            pltpu.VMEM((TOK, D), BF16),
            pltpu.VMEM((1, D), F32),
        ),
        in_specs=[hbm] * 16,
        out_specs=(vmem, vmem),
        scratch_shapes=[
            pltpu.VMEM((TOK, D), BF16),
            pltpu.VMEM((1, D), F32),
            pltpu.VMEM((1, SHARDS), jnp.int32),
            pltpu.VMEM((1, SHARDS), jnp.int32),
            pltpu.VMEM((2, D), BF16),
            pltpu.SMEM((2,), jnp.int32),
            *[pltpu.VMEM(table.shape, table.dtype) for table in consts],
            pltpu.VMEM((3, D, D), BF16),
            pltpu.VMEM((D, D), BF16),
            pltpu.VMEM((2, CH, 128, 128), F32),
            pltpu.VMEM((1024, D), BF16),
            pltpu.VMEM((2, 128, D), F32),
            slab, slab, slab, slab, slab, slab,
            pltpu.VMEM((1032, 128), F32),
            pltpu.VMEM((1032, 128), F32),
            pltpu.VMEM((1032, 128), F32),
            pltpu.VMEM((1032, 128), F32),
            pltpu.VMEM((NZ, 2, QW), BF16),
            pltpu.VMEM((NX, 16, QW), BF16),
            pltpu.VMEM((2, NY, NX, 16, QW), BF16),
            pltpu.VMEM((NY, 32, D), F32),
            pltpu.VMEM((NY, 32, D), F32),
            pltpu.VMEM((NX, NZ, D), F32),
            pltpu.VMEM((NX, NZ, D), F32),
            pltpu.VMEM((NZ, 1, D), F32),
            pltpu.VMEM((NZ, 1, D), F32),
            dma((18,)), dma((3,)), dma((3,)), dma((17,)), dma((17,)), dma((16,)), dma((16,)),
        ],
        compiler_params=pltpu.CompilerParams(
            collective_id=0, has_side_effects=True, vmem_limit_bytes=63 * 2**20
        ),
    )(
        tokens.reshape(TOK, D), norm_gain, proj_weight, out_weight,
        filter_spectrum, span_start, span_end, queries, labels, *consts,
    )
    return layer.reshape(1, 1, TOK, D), grad.reshape(1, 1, D)


def solution(mesh):
    torus = Mesh(mesh.devices.reshape(mesh.shape["doc"], NZ, NX, NY), DOC_SEQ)
    placed = (
        P("doc", SEQ, None, None),
        P(),
        P(),
        P(),
        P(None, SEQ, None, None),
        P("doc", None),
        P("doc", None),
        P(DOC_SEQ, None),
        P(DOC_SEQ),
    )
    return jax.shard_map(
        per_device,
        mesh=torus,
        in_specs=placed,
        out_specs=(P("doc", SEQ, None, None), P("doc", SEQ, None)),
        check_vma=False,
    )
```

```python
import functools
import math

import jax
import jax.numpy as jnp
import ml_dtypes
import numpy as np
from jax import lax
from jax.experimental import pallas as pl
from jax.experimental.pallas import tpu as pltpu
from jax.sharding import Mesh
from jax.sharding import PartitionSpec as P

SEQ = ("seq_0", "seq_1", "seq_2")
DOC_SEQ = ("doc", "seq_0", "seq_1", "seq_2")
MESH = pl.DeviceIdType.MESH

NZ, NX, NY = 8, 4, 4
SHARDS = 128
TOK = 128
D = 768
CH = 6
N = TOK * SHARDS
QW = D + 128
EPS = 1e-06
SCALE = 10.0
OFFSET = -4.0
F32 = jnp.float32
BF16 = jnp.bfloat16


def split_table(table):
    high = table.astype(ml_dtypes.bfloat16)
    low = (table - high.astype(np.float64)).astype(ml_dtypes.bfloat16)
    return high, low


def tables():
    index = np.arange(128)
    angle = 2.0 * math.pi * ((index[:, None] * index[None, :]) % 128) / 128
    cosine, sine = np.cos(angle), np.sin(angle)
    first = np.stack(split_table(np.concatenate([cosine, -sine], axis=1)))
    first = first.reshape(256, 256)
    second = np.stack(split_table(np.block([[cosine, sine], [-sine, cosine]])))
    third = np.stack(split_table(np.block([[cosine, -sine], [sine, cosine]])))
    fourth = np.stack(split_table(np.concatenate([cosine, -sine], axis=0) / N))
    twist = 2.0 * math.pi * (index[:, None] * index[None, :]) / N
    twist = np.stack([np.cos(twist), np.sin(twist)]).astype(np.float32)
    spread = np.zeros((512, 384), np.float32)
    for slot in range(64):
        for row in range(CH):
            spread[8 * slot + row, CH * slot + row] = 1.0
    spread = spread.astype(ml_dtypes.bfloat16)
    return first, second, third, fourth, twist, twist[:, :, None, :], spread


def dot(a, b):
    return jnp.dot(a, b, preferred_element_type=F32)


def halves(value):
    high = value.astype(BF16)
    low = (value - high.astype(F32)).astype(BF16)
    return high, low


def kernel(
    tok_hbm, gain_hbm, pw_hbm, ow_hbm, filt_hbm, start_hbm, end_hbm, q_hbm, lab_hbm,
    f1_hbm, f2_hbm, f3_hbm, f4_hbm, tw_hbm, twx_hbm, spread_hbm,
    out_ref, grad_ref,
    tok_ref, gain_ref, start_ref, end_ref, q_ref, lab_ref,
    f1_ref, f2_ref, f3_ref, f4_ref, tw_ref, twx_ref, spread_ref,
    pw, ow, filt, wpad, filt_t,
    send_s, send_g, recv_s, recv_g, send_2, recv_2,
    a_re, a_im, conv_ref, pool_ref,
    qz, qx, qf,
    p0, ry, p1, rx, p2, rz,
    load_sem, a2a_send, a2a_recv, q_send, q_recv, t_send, t_recv,
):
    d = lax.axis_index("doc")
    z = lax.axis_index("seq_0")
    x = lax.axis_index("seq_1")
    y = lax.axis_index("seq_2")
    me = z * 16 + x * 4 + y

    pairs = [
        (tok_hbm, tok_ref), (gain_hbm, gain_ref.at[0]),
        (pw_hbm.at[:, pl.ds(0, D)], pw.at[0]), (pw_hbm.at[:, pl.ds(D, D)], pw.at[1]),
        (spread_hbm, spread_ref), (pw_hbm.at[:, pl.ds(2 * D, D)], pw.at[2]),
        (q_hbm, q_ref), (lab_hbm, lab_ref), (start_hbm, start_ref), (end_hbm, end_ref),
        (ow_hbm, ow), (filt_hbm, filt), (f1_hbm, f1_ref), (twx_hbm, twx_ref),
        (f2_hbm, f2_ref), (f3_hbm, f3_ref), (tw_hbm, tw_ref), (f4_hbm, f4_ref),
    ]
    loads = [
        pltpu.make_async_copy(src, dst, load_sem.at[slot])
        for slot, (src, dst) in enumerate(pairs)
    ]
    for load in loads[:6]:
        load.start()

    def arrived(*slots):
        for slot in slots:
            loads[slot].wait()

    ring_z = [lax.rem(z + k, NZ) for k in range(NZ)]
    ring_x = [lax.rem(x + k, NX) for k in range(NX)]
    ring_y = [lax.rem(y + k, NY) for k in range(NY)]

    def all_peers(visit):
        def plane(step, carry):
            kz = 4 + lax.div(step + 1, 2) * (1 - 2 * lax.rem(step, 2))
            pz = lax.rem(z + kz, NZ)
            for kx in (2, 1, 3, 0):
                for ky in (2, 1, 3, 0):
                    visit(pz, ring_x[kx], ring_y[ky])
            return carry

        lax.fori_loop(0, NZ - 1, plane, 0)
        for kx in (2, 1, 3, 0):
            for ky in (2, 1, 3, 0):
                if kx or ky:
                    visit(z, ring_x[kx], ring_y[ky])

    barrier = pltpu.get_barrier_semaphore()

    def greet(pz, px, py):
        pl.semaphore_signal(barrier, inc=1, device_id=(d, pz, px, py), device_id_type=MESH)

    all_peers(greet)
    pl.semaphore_signal(barrier, inc=1, device_id=(1 - d, z, x, y), device_id_type=MESH)

    for load in loads[6:]:
        load.start()

    arrived(0, 1)
    tokens = tok_ref[...]
    wide = tokens.astype(F32)
    rms = lax.rsqrt(jnp.mean(wide * wide, axis=1, keepdims=True) + EPS)
    normed = (wide * rms * gain_ref[...]).astype(BF16)

    def q_copy(src, dst, slot, dev):
        return pltpu.make_async_remote_copy(
            src_ref=src, dst_ref=dst, send_sem=q_send.at[slot], recv_sem=q_recv.at[slot],
            device_id=dev, device_id_type=MESH,
        )

    def t_copy(src, dst, slot, dev):
        return pltpu.make_async_remote_copy(
            src_ref=src, dst_ref=dst, send_sem=t_send.at[slot], recv_sem=t_recv.at[slot],
            device_id=dev, device_id_type=MESH,
        )

    arrived(2, 3, 4)
    signal = (dot(normed, pw[0]) * dot(normed, pw[1])).astype(BF16)
    contract = (((1,), (1,)), ((), ()))

    def spread_out(value, target):
        for half in range(2):
            part = lax.dot_general(
                spread_ref[...], value[:, 384 * half : 384 * (half + 1)], contract,
                preferred_element_type=F32,
            )
            target[pl.ds(64 * half, 64)] = part.reshape(64, 8, 128).astype(BF16)

    spread_out(signal, send_s)
    recv_s[me] = send_s[me]

    def a2a(src, dst, slot):
        def send(pz, px, py):
            pltpu.make_async_remote_copy(
                src_ref=src.at[pz * 16 + px * 4 + py], dst_ref=dst.at[me],
                send_sem=a2a_send.at[slot], recv_sem=a2a_recv.at[slot],
                device_id=(d, pz, px, py), device_id_type=MESH,
            ).start()

        all_peers(send)

    def a2a_all(src, dst, slot):
        return pltpu.make_async_remote_copy(
            src_ref=src.at[pl.ds(0, SHARDS - 1)], dst_ref=dst.at[pl.ds(0, SHARDS - 1)],
            send_sem=a2a_send.at[slot], recv_sem=a2a_recv.at[slot],
            device_id=(d, ring_z[1], x, y), device_id_type=MESH,
        )

    arrived(5)
    gate = dot(normed, pw[2]).astype(BF16)
    spread_out(gate, send_g)
    recv_g[me] = send_g[me]

    arrived(6, 7, 8, 9)
    start_row = start_ref[...].astype(F32)
    end_row = end_ref[...].astype(F32)
    row_id = lax.broadcasted_iota(jnp.int32, (128, 128), 0)
    lane_id = lax.broadcasted_iota(jnp.int32, (128, 128), 1)
    wanted = ((row_id & 7) << 4) | (((row_id >> 3) & 3) << 2) | (row_id >> 5)
    pick = lane_id == wanted
    start_col = jnp.sum(jnp.where(pick, start_row, 0.0), axis=1, keepdims=True)
    end_col = jnp.sum(jnp.where(pick, end_row, 0.0), axis=1, keepdims=True)
    position = (lane_id * SHARDS + me).astype(F32)
    member = jnp.where((position >= start_col) & (position < end_col), 1.0, 0.0).astype(BF16)
    p0[...] = dot(member, tokens).reshape(NY, 32, D)
    ry[y] = p0[y]

    qz[z, :, pl.ds(0, D)] = q_ref[...]
    label_row = lax.broadcasted_iota(jnp.int32, (2, 128), 0)
    qz[z, :, pl.ds(D, 128)] = jnp.where(label_row == 0, lab_ref[0], lab_ref[1]).astype(F32).astype(BF16)

    pl.semaphore_wait(barrier, SHARDS)
    q_z = [q_copy(qz.at[z], qz.at[z], k, (d, ring_z[k], x, y)) for k in range(1, NZ)]
    for copy in q_z:
        copy.start()
    t_y = [t_copy(p0.at[ring_y[k]], ry.at[y], k, (d, z, x, ring_y[k])) for k in range(1, NY)]
    for copy in t_y:
        copy.start()

    a2a(send_s, recv_s, 0)
    a2a(send_g, recv_g, 1)
    arrived(10)
    for half in range(2):
        padded = dot(spread_ref[...], ow[pl.ds(384 * half, 384), :])
        wpad[pl.ds(512 * half, 512), :] = padded.astype(BF16)
    arrived(11)
    for part in range(2):
        for e in range(CH):
            filt_t[part, :, pl.ds(128 * e, 128)] = filt[part, e].T
    for e in range(CH, 8):
        conv_ref[pl.ds(e, 128, stride=8), :] = jnp.zeros((128, 128), F32)
    pool_ref[...] = jnp.zeros_like(pool_ref)
    start_hi = start_ref[...] >> 7
    start_lo = start_ref[...] & 127
    end_hi = end_ref[...] >> 7
    end_lo = end_ref[...] & 127
    inside = jnp.where((row_id >= start_hi) & (row_id < end_hi), 1.0, 0.0)
    at_end = jnp.where(row_id == end_hi, 1.0, 0.0)
    at_start = jnp.where(row_id == start_hi, 1.0, 0.0)
    spans = jnp.concatenate([inside, at_end, at_start], axis=1).astype(BF16)

    for copy in q_z:
        copy.wait_recv()
    rows = []
    for block in range(QW // 128):
        for k in range(NZ):
            a_re[pl.ds(16 * block + 2 * k, 2), :] = qz[k, :, pl.ds(128 * block, 128)].astype(F32)
        rows.append(a_re[pl.ds(16 * block, 16), :].astype(BF16))
    qx[x] = jnp.concatenate(rows, axis=1)
    q_x = [q_copy(qx.at[x], qx.at[x], 8 + k, (d, z, ring_x[k], y)) for k in range(1, NX)]
    for copy in q_x:
        copy.start()

    for copy in t_y:
        copy.wait_recv()
    p1[...] = ((ry[0] + ry[1]) + (ry[2] + ry[3])).reshape(NX, NZ, D)
    rx[x] = p1[x]
    t_x = [t_copy(p1.at[ring_x[k]], rx.at[x], 4 + k, (d, z, ring_x[k], y)) for k in range(1, NX)]
    for copy in t_x:
        copy.start()

    arrived(12, 13, 14, 15, 16, 17)
    a2a_all(send_s, recv_s, 0).wait_recv()
    got = recv_s[...].astype(F32).reshape(1024, 128).astype(BF16)
    spec = dot(jnp.concatenate([got, got], axis=1), f1_ref[...])
    spec_re = spec[:, :128].reshape(128, 8, 128)
    spec_im = spec[:, 128:].reshape(128, 8, 128)
    cos_x, sin_x = twx_ref[0], twx_ref[1]
    a_re[pl.ds(0, 1024), :] = (spec_re * cos_x + spec_im * sin_x).reshape(1024, 128)
    a_im[pl.ds(0, 1024), :] = (spec_im * cos_x - spec_re * sin_x).reshape(1024, 128)

    def columns(ref):
        return jnp.concatenate(
            [ref[pl.ds(e, 128, stride=8), :] for e in range(CH)], axis=1
        )

    def triple(left_ref, value):
        high, low = halves(value)
        return dot(left_ref[0], high) + (dot(left_ref[0], low) + dot(left_ref[1], high))

    full = triple(f2_ref, jnp.concatenate([columns(a_re), columns(a_im)], axis=0))
    full_re, full_im = full[:128], full[128:]
    h_re, h_im = filt_t[0], filt_t[1]
    prod = jnp.concatenate(
        [full_re * h_re - full_im * h_im, full_re * h_im + full_im * h_re], axis=0
    )
    back = triple(f3_ref, prod)
    back_re, back_im = back[:128], back[128:]
    cos_t, sin_t = tw_ref[0], tw_ref[1]
    turned = []
    for e in range(CH):
        e_re = back_re[:, 128 * e : 128 * (e + 1)]
        e_im = back_im[:, 128 * e : 128 * (e + 1)]
        turned.append(
            jnp.concatenate([e_re * cos_t - e_im * sin_t, e_re * sin_t + e_im * cos_t], axis=1)
        )
    high, low = halves(jnp.concatenate(turned, axis=0))
    conv = dot(high, f4_ref[0]) + (dot(low, f4_ref[0]) + dot(high, f4_ref[1]))
    for e in range(CH):
        conv_ref[pl.ds(e, 128, stride=8), :] = conv[128 * e : 128 * (e + 1)]

    for copy in q_x:
        copy.wait_recv()
    qf[d, y] = qx[...]
    q_y = [q_copy(qx, qf.at[d, y], 12 + k, (d, z, x, ring_y[k])) for k in range(1, NY)]
    for copy in q_y:
        copy.start()

    for copy in t_x:
        copy.wait_recv()
    total_z = (rx[0] + rx[1]) + (rx[2] + rx[3])
    for k in range(NZ):
        p2[k] = total_z[k : k + 1]
    rz[z] = p2[z]
    t_z = [t_copy(p2.at[ring_z[k]], rz.at[z], 8 + k, (d, ring_z[k], x, y)) for k in range(1, NZ)]
    for copy in t_z:
        copy.start()

    a2a_all(send_g, recv_g, 1).wait_recv()
    gated = (recv_g[...].astype(F32) * conv_ref[pl.ds(0, 1024), :].reshape(128, 8, 128)).astype(BF16)
    gated_wide = gated.astype(F32).reshape(1024, 128)
    sums = dot(gated_wide.astype(BF16), spans)
    shard_id = lax.broadcasted_iota(jnp.int32, (128, 1, 128), 0)
    below_end = jnp.where(shard_id < end_lo.reshape(1, 1, 128), 1.0, 0.0)
    below_start = jnp.where(shard_id < start_lo.reshape(1, 1, 128), 1.0, 0.0)
    pooled_t = jnp.sum(
        sums[:, :128].reshape(128, 8, 128)
        + below_end * sums[:, 128:256].reshape(128, 8, 128)
        - below_start * sums[:, 256:].reshape(128, 8, 128),
        axis=0,
    )
    piece_0 = pooled_t.astype(BF16).astype(F32)
    rest = pooled_t - piece_0
    piece_1 = rest.astype(BF16).astype(F32)
    piece_2 = rest - piece_1
    pieces = jnp.concatenate(
        [piece_0, piece_1, piece_2, jnp.zeros((104, 128), F32)], axis=0
    ).T
    pool_ref[pl.ds(CH, 128, stride=8), :] = pieces
    send_2[...] = (gated_wide + pool_ref[pl.ds(0, 1024), :]).reshape(128, 8, 128).astype(BF16)
    recv_2[me] = send_2[me]
    a2a(send_2, recv_2, 2)

    for copy in q_y:
        copy.wait_recv()
    q_d = q_copy(qf.at[d], qf.at[d], 16, (1 - d, z, x, y))
    q_d.start()
    q_d.wait_recv()

    queries = qf[...].reshape(512, QW)
    wide_q = queries[:, :D].astype(F32)
    label_col = queries[:, D : D + 1].astype(F32)
    q_inv = lax.rsqrt(jnp.sum(wide_q * wide_q, axis=1, keepdims=True) + EPS)
    for copy in t_z:
        copy.wait_recv()
    token_sum = jnp.sum(rz[...], axis=0)
    mine = lax.broadcasted_iota(jnp.int32, (1, 128), 1) == me
    count = jnp.sum(jnp.where(mine, end_row - start_row, 0.0), axis=1, keepdims=True)

    a2a_all(send_2, recv_2, 2).wait_recv()
    back_rows = recv_2[...].astype(F32)
    row_in = lax.broadcasted_iota(jnp.int32, (1, 8, 128), 1)
    lane_in = lax.broadcasted_iota(jnp.int32, (1, 8, 128), 2)
    own_lane = ((lane_in & 7) == row_in) & (lane_in < 24)
    pool_rows = jnp.where(own_lane, back_rows[:, CH : CH + 1, :], 0.0)
    both = jnp.concatenate(
        [back_rows.reshape(1024, 128), pool_rows.reshape(1024, 128)[:, :32]], axis=1
    ).astype(BF16)
    mixed = lax.dot_general(
        both, wpad[...], (((0,), (0,)), ((), ())), preferred_element_type=F32
    )
    out_ref[...] = (mixed[:128] + wide).astype(BF16)

    pooled = (token_sum + jnp.sum(mixed[128:152], axis=0, keepdims=True)) / count
    inv = lax.rsqrt(jnp.sum(pooled * pooled, axis=1, keepdims=True) + EPS)
    unit = pooled * inv
    logits = SCALE * (jnp.sum(wide_q * unit, axis=1, keepdims=True) * q_inv) + OFFSET
    passage = (d * 128 + me).astype(F32)
    sign = jnp.where(label_col == passage, 1.0, -1.0)
    weight = -sign / (1.0 + jnp.exp(sign * logits))
    unit_grad = SCALE * jnp.sum((weight * q_inv) * wide_q, axis=0, keepdims=True)
    radial = jnp.sum(unit * unit_grad, axis=1, keepdims=True)
    grad_ref[...] = inv * (unit_grad - unit * radial)

    for src, dst, slot in ((send_s, recv_s, 0), (send_g, recv_g, 1), (send_2, recv_2, 2)):
        a2a_all(src, dst, slot).wait_send()
    for copy in q_z + q_x + q_y + [q_d] + t_y + t_x + t_z:
        copy.wait_send()


def per_device(
    tokens, norm_gain, proj_weight, out_weight, filter_spectrum,
    span_start, span_end, queries, labels,
):
    vmem = pl.BlockSpec(memory_space=pltpu.VMEM)
    hbm = pl.BlockSpec(memory_space=pl.ANY)
    consts = [jnp.asarray(table) for table in tables()]
    dma = pltpu.SemaphoreType.DMA
    slab = pltpu.VMEM((SHARDS, 8, 128), BF16)
    layer, grad = pl.pallas_call(
        kernel,
        name="layer",
        out_shape=(
            pltpu.VMEM((TOK, D), BF16),
            pltpu.VMEM((1, D), F32),
        ),
        in_specs=[hbm] * 16,
        out_specs=(vmem, vmem),
        scratch_shapes=[
            pltpu.VMEM((TOK, D), BF16),
            pltpu.VMEM((1, D), F32),
            pltpu.VMEM((1, SHARDS), jnp.int32),
            pltpu.VMEM((1, SHARDS), jnp.int32),
            pltpu.VMEM((2, D), BF16),
            pltpu.SMEM((2,), jnp.int32),
            *[pltpu.VMEM(table.shape, table.dtype) for table in consts],
            pltpu.VMEM((3, D, D), BF16),
            pltpu.VMEM((D, D), BF16),
            pltpu.VMEM((2, CH, 128, 128), F32),
            pltpu.VMEM((1024, D), BF16),
            pltpu.VMEM((2, 128, D), F32),
            slab, slab, slab, slab, slab, slab,
            pltpu.VMEM((1032, 128), F32),
            pltpu.VMEM((1032, 128), F32),
            pltpu.VMEM((1032, 128), F32),
            pltpu.VMEM((1032, 128), F32),
            pltpu.VMEM((NZ, 2, QW), BF16),
            pltpu.VMEM((NX, 16, QW), BF16),
            pltpu.VMEM((2, NY, NX, 16, QW), BF16),
            pltpu.VMEM((NY, 32, D), F32),
            pltpu.VMEM((NY, 32, D), F32),
            pltpu.VMEM((NX, NZ, D), F32),
            pltpu.VMEM((NX, NZ, D), F32),
            pltpu.VMEM((NZ, 1, D), F32),
            pltpu.VMEM((NZ, 1, D), F32),
            dma((18,)), dma((3,)), dma((3,)), dma((17,)), dma((17,)), dma((16,)), dma((16,)),
        ],
        compiler_params=pltpu.CompilerParams(
            collective_id=0, has_side_effects=True, vmem_limit_bytes=63 * 2**20
        ),
    )(
        tokens.reshape(TOK, D), norm_gain, proj_weight, out_weight,
        filter_spectrum, span_start, span_end, queries, labels, *consts,
    )
    return layer.reshape(1, 1, TOK, D), grad.reshape(1, 1, D)


def solution(mesh):
    torus = Mesh(mesh.devices.reshape(mesh.shape["doc"], NZ, NX, NY), DOC_SEQ)
    placed = (
        P("doc", SEQ, None, None),
        P(),
        P(),
        P(),
        P(None, SEQ, None, None),
        P("doc", None),
        P("doc", None),
        P(DOC_SEQ, None),
        P(DOC_SEQ),
    )
    return jax.shard_map(
        per_device,
        mesh=torus,
        in_specs=placed,
        out_specs=(P("doc", SEQ, None, None), P("doc", SEQ, None)),
        check_vma=False,
    )
```
